32 devices in a mesh: seqlo: 8 (over z, y), seqhi: 4 (over x, core).
Axes of the slice: x: 2, y: 2, z: 4, core: 2. Of those that a mesh axis runs over, the one named last changes fastest.
Arguments:
- waveform_input: bfloat16 [65536, 256], P(('seqhi', 'seqlo')), may hold values from -6 to 6
- first_conv_weight: bfloat16 [512, 512], P('seqhi'), may hold values from -0.25 to 0.25
- first_projection_weight: bfloat16 [256, 256], P('seqhi'), may hold values from -0.375 to 0.375
- second_conv_weight: bfloat16 [512, 512], P('seqhi'), may hold values from -0.25 to 0.25
- second_projection_weight: bfloat16 [256, 256], P('seqhi'), may hold values from -0.375 to 0.375
- final_cotangent: bfloat16 [65536, 256], P(('seqhi', 'seqlo')), may hold values from -6 to 6
Outputs:
- input_cotangent: bfloat16 [65536, 256], P(('seqhi', 'seqlo'))
- first_conv_gradient: float32 [512, 512], P('seqhi')
- first_projection_gradient: float32 [256, 256], P('seqhi')
- second_conv_gradient: float32 [512, 512], P('seqhi')
- second_projection_gradient: float32 [256, 256], P('seqhi')
The draws below stay inside these ranges and needn't reach their ends.
All inputs are finite; a program needn't handle non-finite values.
Results may differ from the reference program's by a relative error of at most 0.0062.
Values may be sent and summed in bfloat16 or wider, within the bound.
A program may use at most 64 MiB of HBM per device.

```python
import jax
import jax.numpy as jnp
from jax import lax

R = 256
H = 512
G = 256
SEQ = 65536
DILATION_FIRST1 = 16384
DILATION_SECOND2 = 32768


def block_levels(rng, dims, pieces, least, high):
    level, own = 1.0, jax.random.fold_in(rng, 6)
    for axis_at, blocks in pieces:
        steps = jnp.exp(jax.random.uniform(jax.random.fold_in(own, axis_at), (blocks,), jnp.float32, least / len(pieces), high / len(pieces)))
        level = level * jnp.repeat(steps, dims[axis_at] // blocks).reshape([-1 if axis == axis_at else 1 for axis in range(len(dims))])
    return level


def scatter_about(key, shape, spread, limit, cuts=(), held_as=jnp.bfloat16):
    array = jax.random.normal(key, shape, jnp.float32) * spread
    if len(cuts) > 0:
        array = block_levels(key, shape, cuts, -0.22, 0.18) * array
    return jnp.clip(array, min=-limit, max=limit).astype(held_as)


def setup_inputs(seed: int = 0) -> dict:
    splits = jax.random.split(jax.random.key(seed), 7)
    waveform_input = scatter_about(splits[0], (SEQ, R), 1.0, 6.0, ((0, 32),))
    first_conv_weight = scatter_about(splits[1], (2 * R, H), (2 * R) ** -0.5, 0.25, ((0, 4),))
    first_projection_weight = scatter_about(splits[2], (G, R), G ** -0.5, 0.375, ((0, 4),))
    second_conv_weight = scatter_about(splits[3], (2 * R, H), (2 * R) ** -0.5, 0.25, ((0, 4),))
    second_projection_weight = scatter_about(splits[4], (G, R), G ** -0.5, 0.375, ((0, 4),))
    final_cotangent = scatter_about(splits[5], (SEQ, R), 1.0, 6.0, ((0, 32),))
    return dict(waveform_input=waveform_input, first_conv_weight=first_conv_weight, first_projection_weight=first_projection_weight, second_conv_weight=second_conv_weight, second_projection_weight=second_projection_weight, final_cotangent=final_cotangent)


def layer_forward_step(layer_input, conv_weight, projection_weight, dilation_span):
    channel_width = layer_input.shape[1]
    earlier_samples = jnp.concatenate([jnp.zeros((dilation_span, channel_width), jnp.bfloat16), layer_input[:-dilation_span]], 0)
    stacked_taps = jnp.concatenate([earlier_samples, layer_input], 1)
    gated_mixture = jnp.dot(stacked_taps, conv_weight, preferred_element_type=jnp.float32)
    half = conv_weight.shape[1] // 2
    hidden_state = (jnp.tanh(gated_mixture[:, :half]) * jax.nn.sigmoid(gated_mixture[:, half:])).astype(jnp.bfloat16)
    output = (layer_input.astype(jnp.float32) + jnp.dot(hidden_state, projection_weight, preferred_element_type=jnp.float32)).astype(jnp.bfloat16)
    return output, stacked_taps, gated_mixture, hidden_state


def layer_backward_step(output_cotangent, stacked_taps, gated_mixture, hidden_state, conv_weight, projection_weight, dilation_span, gradient_scale):
    channel_width = output_cotangent.shape[1]
    half = conv_weight.shape[1] // 2
    dhid = lax.dot_general(output_cotangent, projection_weight, (((1,), (1,)), ((), ())), preferred_element_type=jnp.float32)
    grad_outw = lax.dot_general(hidden_state, output_cotangent, (((0,), (0,)), ((), ())), preferred_element_type=jnp.float32) * gradient_scale
    tanh_part = jnp.tanh(gated_mixture[:, :half])
    sig_part = jax.nn.sigmoid(gated_mixture[:, half:])
    dmixed = jnp.concatenate([dhid * sig_part * (1.0 - tanh_part * tanh_part), dhid * tanh_part * sig_part * (1.0 - sig_part)], 1).astype(jnp.bfloat16)
    grad_filt = lax.dot_general(stacked_taps, dmixed, (((0,), (0,)), ((), ())), preferred_element_type=jnp.float32) * gradient_scale
    dstack = lax.dot_general(dmixed, conv_weight, (((1,), (1,)), ((), ())), preferred_element_type=jnp.float32)
    tap_position = lax.optimization_barrier(dstack[:, :channel_width].astype(jnp.bfloat16))
    later_samples = jnp.concatenate([tap_position[dilation_span:], jnp.zeros((dilation_span, channel_width), jnp.bfloat16)], 0)
    cot_prev = (output_cotangent.astype(jnp.float32) + dstack[:, channel_width:] + later_samples.astype(jnp.float32)).astype(jnp.bfloat16)
    return cot_prev, grad_filt, grad_outw


def reference(waveform_input, first_conv_weight, first_projection_weight, second_conv_weight, second_projection_weight, final_cotangent):
    gradient_scale = jnp.float32(SEQ) ** -0.5
    second_layer_input, first_stacked_taps, first_gated_mixture, first_hidden_state = layer_forward_step(waveform_input, first_conv_weight, first_projection_weight, DILATION_FIRST1)
    ignored_value, second_stacked_taps, second_gated_mixture, second_hidden_state = layer_forward_step(second_layer_input, second_conv_weight, second_projection_weight, DILATION_SECOND2)
    middle_cotangent, second_conv_gradient, second_projection_gradient = layer_backward_step(final_cotangent, second_stacked_taps, second_gated_mixture, second_hidden_state, second_conv_weight, second_projection_weight, DILATION_SECOND2, gradient_scale)
    input_cotangent, first_conv_gradient, first_projection_gradient = layer_backward_step(middle_cotangent, first_stacked_taps, first_gated_mixture, first_hidden_state, first_conv_weight, first_projection_weight, DILATION_FIRST1, gradient_scale)
    return input_cotangent, first_conv_gradient, first_projection_gradient, second_conv_gradient, second_projection_gradient
```

```python
import functools

import jax
import jax.numpy as jnp
from jax import lax
from jax.experimental import pallas as pl
from jax.experimental.pallas import tpu as pltpu
from jax.sharding import PartitionSpec as P

F32, BF16 = jnp.float32, jnp.bfloat16
MESH = pl.DeviceIdType.MESH


def flip(index, bits):
    b = 1
    while b <= bits:
        if bits & b:
            index = index + b - 2 * b * lax.rem(lax.div(index, b), 2)
        b *= 2
    return index


def dot(a, b):
    return jnp.dot(a, b, preferred_element_type=F32)


def dot_rows(a, b):
    return lax.dot_general(a, b, (((0,), (0,)), ((), ())), preferred_element_type=F32)


def dot_cols(a, b):
    return lax.dot_general(a, b, (((1,), (1,)), ((), ())), preferred_element_type=F32)


def sigmoid(v):
    return 0.5 * jnp.tanh(0.5 * v) + 0.5


def kernel(
    nhi, nlo, chunks, scale,
    x_in, f1_in, p1_in, f2_in, p2_in, c_in,
    y_out, gf1_out, gp1_out, gf2_out, gp2_out,
    wf1, wp1, wf2, wp2, xs, cs, ys, t1, s1, h1, c1,
    gf1, gp1, gf2, gp2, g32, gb, rb, lb, lr, ag,
    w_send, w_recv, w_own, x_send, x_recv, c_send, c_recv, y_send, y_recv, own,
    h_send, h_recv, l_send, l_recv, a_send, a_recv,
):
    hi, lo = lax.axis_index("seqhi"), lax.axis_index("seqlo")
    m, width = xs.shape[1], xs.shape[2]
    mc = m // chunks
    half = width
    r, rp = f1_in.shape[0], p1_in.shape[0]
    fcols, pcols = f1_in.shape[1] // 128, p1_in.shape[1] // 128
    length = g32.shape[2]
    piece = lr.shape[2]

    def remote(src, dst, send, recv, axis, partner):
        return pltpu.make_async_remote_copy(
            src_ref=src, dst_ref=dst, send_sem=send, recv_sem=recv,
            device_id={axis: partner}, device_id_type=MESH,
        )

    barrier = pltpu.get_barrier_semaphore()
    for j in range(1, nhi):
        pl.semaphore_signal(barrier, inc=1, device_id={"seqhi": flip(hi, j)}, device_id_type=MESH)
    for j in range(1, nlo):
        pl.semaphore_signal(barrier, inc=1, device_id={"seqlo": flip(lo, j)}, device_id_type=MESH)

    inputs = (f1_in, p1_in, f2_in, p2_in)
    full = (wf1, wp1, wf2, wp2)
    local_copies = []
    for a in range(4):
        size = inputs[a].shape[0]
        here = pl.ds(pl.multiple_of(hi * size, size), size)
        local_copies.append(pltpu.make_async_copy(inputs[a], full[a].at[here], w_own.at[a]))
    mine = pl.ds(pl.multiple_of(hi * m, m), m)
    local_copies.append(pltpu.make_async_copy(x_in.at[mine], xs.at[hi], w_own.at[4]))
    local_copies.append(pltpu.make_async_copy(c_in.at[mine], cs.at[hi], w_own.at[5]))
    for copy in local_copies:
        copy.start()

    pl.semaphore_wait(barrier, nhi - 1 + nlo - 1)

    bits = []
    b = nhi // 2
    while b >= 1:
        bits.append(b)
        b //= 2
    plan = []
    held = [0]
    for b in bits:
        for h in held:
            plan.append((h, b))
        held = held + [h ^ b for h in held]

    def weight_copy(a, at):
        h, b = plan[at]
        size = inputs[a].shape[0]
        there = pl.ds(pl.multiple_of(flip(hi, h) * size, size), size)
        src = inputs[a] if h == 0 else full[a].at[there]
        return remote(src, full[a].at[there], w_send.at[a, at], w_recv.at[a, at], "seqhi", flip(hi, b))

    def sample_copy(src, dst, send, recv, j, k):
        partner = flip(hi, j)
        start = pl.multiple_of(partner * m + k * mc, mc)
        part = pl.ds(pl.multiple_of(k * mc, mc), mc)
        return remote(src.at[pl.ds(start, mc)], dst.at[hi, part], send.at[j, k], recv.at[j, k], "seqhi", partner)

    def x_copy(j, k):
        return sample_copy(x_in, xs, x_send, x_recv, j, k)

    def c_copy(j, k):
        return sample_copy(c_in, cs, c_send, c_recv, j, k)

    for a in range(4):
        for at in range(len(plan)):
            if plan[at][0] == 0:
                weight_copy(a, at).start()
    for k in range(chunks):
        for j in range(nhi - 1, 0, -1):
            x_copy(j, k).start()
        for j in range(nhi - 1, 0, -1):
            c_copy(j, k).start()

    for ref in (gf1, gp1, gf2, gp2):
        ref[...] = jnp.zeros_like(ref)
    if length > r * fcols + rp * pcols:
        g32[...] = jnp.zeros_like(g32)
        gb[...] = jnp.zeros_like(gb)

    for copy in local_copies:
        copy.wait()
    arrived = {h ^ b: at for at, (h, b) in enumerate(plan)}
    for a in range(4):
        waited = set()
        for at, (h, b) in enumerate(plan):
            if h:
                if arrived[h] not in waited:
                    weight_copy(a, arrived[h]).wait_recv()
                    waited.add(arrived[h])
                weight_copy(a, at).start()
        for at in range(len(plan)):
            if at not in waited:
                weight_copy(a, at).wait_recv()

    def gates(mixed):
        return jnp.tanh(mixed[:, :half]), sigmoid(mixed[:, half:])

    def mix(v, weight, steps):
        cut = steps * mc
        current = dot(v, weight[width:, :])
        delayed = dot(v[:-cut], weight[:width, :])
        return jnp.concatenate([current[:cut], current[cut:] + delayed], 0)

    def back(v, c, t, s, hidden, weight, projection, gf, gp, steps):
        cut = steps * mc
        dhid = dot_cols(c, projection[...])
        gp[...] += dot_rows(hidden, c)
        dmixed = jnp.concatenate(
            [dhid * s * (1.0 - t * t), dhid * t * s * (1.0 - s)], 1
        ).astype(BF16)
        gf[width:, :] += dot_rows(v, dmixed)
        gf[:width, :] += dot_rows(v[:-cut], dmixed[cut:])
        current = c.astype(F32) + dot_cols(dmixed, weight[width:, :])
        tap = dot_cols(dmixed[cut:], weight[:width, :]).astype(BF16).astype(F32)
        return jnp.concatenate([current[:-cut] + tap, current[-cut:]], 0).astype(BF16)

    rows = nhi * mc

    def first_loop(k, carry):
        part = pl.ds(pl.multiple_of(k * mc, mc), mc)
        for j in range(1, nhi):
            x_copy(j, k).wait_recv()
        x = xs[:, part, :].reshape(rows, width)
        t, s = gates(mix(x, wf1, 1))
        hidden = (t * s).astype(BF16)
        t1[k], s1[k], h1[k] = t, s, hidden
        x2 = (x.astype(F32) + dot(hidden, wp1[...])).astype(BF16)
        t, s = gates(mix(x2, wf2, 2))
        hidden = (t * s).astype(BF16)
        for j in range(1, nhi):
            c_copy(j, k).wait_recv()
        c = cs[:, part, :].reshape(rows, width)
        c1[k] = back(x2, c, t, s, hidden, wf2, wp2, gf2, gp2, 2)
        return carry

    lax.fori_loop(0, chunks, first_loop, 0)

    def pack(layer):
        gf, gp = (gf1, gp1) if layer == 0 else (gf2, gp2)
        for j in range(nhi):
            q = flip(hi, j)
            f_rows = pl.ds(pl.multiple_of(q * r, r), r)
            p_rows = pl.ds(pl.multiple_of(q * rp, rp), rp)
            for i in range(fcols + pcols):
                if i < fcols:
                    values = gf[f_rows, i * 128:(i + 1) * 128]
                    at = slice(i * r, (i + 1) * r)
                else:
                    col = i - fcols
                    values = gp[p_rows, col * 128:(col + 1) * 128]
                    at = slice(fcols * r + col * rp, fcols * r + (col + 1) * rp)
                if j & 1:
                    gb[layer, j, at, :] = values.astype(BF16)
                else:
                    g32[layer, j, at, :] = values

    def hi_copy(layer, j):
        b = j & -j
        return remote(
            gb.at[layer, j], rb.at[layer, j], h_send.at[layer, j], h_recv.at[layer, j],
            "seqhi", flip(hi, b),
        )

    def hi_slots(s):
        return [j for j in range(nhi) if j & -j == 1 << s]

    def hi_start(layer, s):
        for j in hi_slots(s):
            hi_copy(layer, j).start()

    def hi_finish(layer, s):
        for j in hi_slots(s):
            hi_copy(layer, j).wait_recv()
            target = j ^ (1 << s)
            total = g32[layer, target] + rb[layer, j].astype(F32)
            g32[layer, target] = total
            if target and target & -target == 2 << s:
                gb[layer, target] = total.astype(BF16)

    def piece_at(index):
        return pl.ds(pl.multiple_of(index * piece, piece), piece)

    def lo_copy(layer, j):
        partner = flip(lo, j)
        return remote(
            lb.at[layer, piece_at(partner)], lr.at[layer, j], l_send.at[layer, j],
            l_recv.at[layer, j], "seqlo", partner,
        )

    def lo_start(layer):
        lb[layer] = g32[layer, 0].astype(BF16)
        for j in range(nlo - 1, 0, -1):
            lo_copy(layer, j).start()

    def ag_copy(layer, j):
        return remote(
            ag.at[layer, piece_at(lo)], ag.at[layer, piece_at(lo)], a_send.at[layer, j],
            a_recv.at[layer, j], "seqlo", flip(lo, j),
        )

    def lo_finish(layer):
        total = g32[layer, 0, piece_at(lo), :]
        for j in range(1, nlo):
            lo_copy(layer, j).wait_recv()
            total = total + lr[layer, j].astype(F32)
        ag[layer, piece_at(lo), :] = (total * scale).astype(BF16)
        for j in range(nlo - 1, 0, -1):
            ag_copy(layer, j).start()

    def ag_finish(layer):
        gf, gp = (gf1_out, gp1_out) if layer == 0 else (gf2_out, gp2_out)
        for j in range(1, nlo):
            ag_copy(layer, j).wait_recv()
        for i in range(fcols):
            gf[:, i * 128:(i + 1) * 128] = ag[layer, i * r:(i + 1) * r, :].astype(F32)
        for i in range(pcols):
            at = fcols * r + i * rp
            gp[:, i * 128:(i + 1) * 128] = ag[layer, at:at + rp, :].astype(F32)

    stages = len(bits)

    def phases(layer):
        steps = []
        for s in range(stages):
            def step(s=s):
                hi_finish(layer, s)
                if s + 1 < stages:
                    hi_start(layer, s + 1)
                else:
                    lo_start(layer)
            steps.append(step)
        steps.append(lambda: lo_finish(layer))
        return steps

    def y_copy(j, k):
        partner = flip(hi, j)
        start = pl.multiple_of(hi * m + k * mc, mc)
        part = pl.ds(pl.multiple_of(k * mc, mc), mc)
        return remote(
            ys.at[partner, part], y_out.at[pl.ds(start, mc)], y_send.at[j, k], y_recv.at[j, k],
            "seqhi", partner,
        )

    def y_local(k):
        start = pl.multiple_of(hi * m + k * mc, mc)
        part = pl.ds(pl.multiple_of(k * mc, mc), mc)
        return pltpu.make_async_copy(ys.at[hi, part], y_out.at[pl.ds(start, mc)], own.at[k])

    pack(1)
    hi_start(1, 0)
    second = phases(1)

    def second_loop(k, carry):
        part = pl.ds(pl.multiple_of(k * mc, mc), mc)
        x = xs[:, part, :].reshape(rows, width)
        y = back(x, c1[k], t1[k], s1[k], h1[k], wf1, wp1, gf1, gp1, 1)
        ys[:, part, :] = y.reshape(nhi, mc, width)
        for j in range(nhi - 1, 0, -1):
            y_copy(j, k).start()
        y_local(k).start()
        for i in range(min(len(second), chunks)):
            pl.when(k == i)(second[i])
        return carry

    lax.fori_loop(0, chunks, second_loop, 0)

    pack(0)
    hi_start(0, 0)
    for step in second[chunks:]:
        step()
    for step in phases(0):
        step()
    ag_finish(1)
    ag_finish(0)

    for a in range(4):
        for at in range(len(plan)):
            weight_copy(a, at).wait_send()
    for k in range(chunks):
        for j in range(1, nhi):
            x_copy(j, k).wait_send()
            c_copy(j, k).wait_send()
            y_copy(j, k).wait()
        y_local(k).wait()
    for layer in range(2):
        for j in range(1, nhi):
            hi_copy(layer, j).wait_send()
        for j in range(1, nlo):
            lo_copy(layer, j).wait_send()
            ag_copy(layer, j).wait_send()


def local(x, f1, p1, f2, p2, c):
    nhi, nlo = lax.axis_size("seqhi"), lax.axis_size("seqlo")
    samples, width = x.shape
    chunks = 4
    m = samples // nhi
    mc = m // chunks
    scale = float(samples * nhi * nlo) ** -0.5
    r, h = f1.shape
    rp = p1.shape[0]
    need = r * (h // 128) + rp * (width // 128)
    piece = -(-need // (16 * nlo)) * 16
    length = piece * nlo
    rows = nhi * mc
    dma = pltpu.SemaphoreType.DMA
    any_spec = pl.BlockSpec(memory_space=pl.ANY)
    vmem = pl.BlockSpec(memory_space=pltpu.VMEM)
    shape = jax.ShapeDtypeStruct
    return pl.pallas_call(
        functools.partial(kernel, nhi, nlo, chunks, scale),
        out_shape=(
            shape(x.shape, BF16), shape(f1.shape, F32), shape(p1.shape, F32),
            shape(f2.shape, F32), shape(p2.shape, F32),
        ),
        in_specs=[any_spec] * 6,
        out_specs=(any_spec, vmem, vmem, vmem, vmem),
        scratch_shapes=[
            pltpu.VMEM((r * nhi, h), BF16),
            pltpu.VMEM((rp * nhi, width), BF16),
            pltpu.VMEM((r * nhi, h), BF16),
            pltpu.VMEM((rp * nhi, width), BF16),
            pltpu.VMEM((nhi, m, width), BF16),
            pltpu.VMEM((nhi, m, width), BF16),
            pltpu.VMEM((nhi, m, width), BF16),
            pltpu.VMEM((chunks, rows, h // 2), F32),
            pltpu.VMEM((chunks, rows, h // 2), F32),
            pltpu.VMEM((chunks, rows, h // 2), BF16),
            pltpu.VMEM((chunks, rows, width), BF16),
            pltpu.VMEM((r * nhi, h), F32),
            pltpu.VMEM((rp * nhi, width), F32),
            pltpu.VMEM((r * nhi, h), F32),
            pltpu.VMEM((rp * nhi, width), F32),
            pltpu.VMEM((2, nhi, length, 128), F32),
            pltpu.VMEM((2, nhi, length, 128), BF16),
            pltpu.VMEM((2, nhi, length, 128), BF16),
            pltpu.VMEM((2, length, 128), BF16),
            pltpu.VMEM((2, nlo, piece, 128), BF16),
            pltpu.VMEM((2, length, 128), BF16),
            dma((4, nhi)), dma((4, nhi)), dma((6,)),
            dma((nhi, chunks)), dma((nhi, chunks)),
            dma((nhi, chunks)), dma((nhi, chunks)),
            dma((nhi, chunks)), dma((nhi, chunks)), dma((chunks,)),
            dma((2, nhi)), dma((2, nhi)),
            dma((2, nlo)), dma((2, nlo)),
            dma((2, nlo)), dma((2, nlo)),
        ],
        compiler_params=pltpu.CompilerParams(
            collective_id=0, has_side_effects=True, vmem_limit_bytes=48 * 1024 * 1024
        ),
        cost_estimate=pl.CostEstimate(
            flops=16 * samples * width * h * 2, bytes_accessed=8 * samples * width,
            transcendentals=4 * samples * h,
        ),
    )(x, f1, p1, f2, p2, c)


def solution(mesh):
    rows = P(("seqhi", "seqlo"), None)
    weights = P("seqhi", None)
    return jax.shard_map(
        local,
        mesh=mesh,
        in_specs=(rows, weights, weights, weights, weights, rows),
        out_specs=(rows, weights, weights, weights, weights),
        check_vma=False,
    )
```

```python
import functools

import jax
import jax.numpy as jnp
from jax import lax
from jax.experimental import pallas as pl
from jax.experimental.pallas import tpu as pltpu
from jax.sharding import PartitionSpec as P

F32, BF16 = jnp.float32, jnp.bfloat16
MESH = pl.DeviceIdType.MESH


def flip(index, bits):
    b = 1
    while b <= bits:
        if bits & b:
            index = index + b - 2 * b * lax.rem(lax.div(index, b), 2)
        b *= 2
    return index


def dot(a, b):
    return jnp.dot(a, b, preferred_element_type=F32)


def dot_rows(a, b):
    return lax.dot_general(a, b, (((0,), (0,)), ((), ())), preferred_element_type=F32)


def dot_cols(a, b):
    return lax.dot_general(a, b, (((1,), (1,)), ((), ())), preferred_element_type=F32)


def sigmoid(v):
    return 0.5 * jnp.tanh(0.5 * v) + 0.5


def kernel(
    nhi, nlo, chunks, scale,
    x_in, f1_in, p1_in, f2_in, p2_in, c_in,
    y_out, gf1_out, gp1_out, gf2_out, gp2_out,
    wf1, wp1, wf2, wp2, xs, cs, ys,
    gf1, gp1, gf2, gp2, g32, gb, rb, lb, lr, ag,
    w_send, w_recv, w_own, x_send, x_recv, c_send, c_recv, y_send, y_recv, own,
    h_send, h_recv, l_send, l_recv, a_send, a_recv,
):
    hi, lo = lax.axis_index("seqhi"), lax.axis_index("seqlo")
    m, width = xs.shape[1], xs.shape[2]
    mc = m // chunks
    half = width
    r, rp = f1_in.shape[0], p1_in.shape[0]
    fcols, pcols = f1_in.shape[1] // 128, p1_in.shape[1] // 128
    length = g32.shape[2]
    piece = lr.shape[2]

    def remote(src, dst, send, recv, axis, partner):
        return pltpu.make_async_remote_copy(
            src_ref=src, dst_ref=dst, send_sem=send, recv_sem=recv,
            device_id={axis: partner}, device_id_type=MESH,
        )

    barrier = pltpu.get_barrier_semaphore()
    for j in range(1, nhi):
        pl.semaphore_signal(barrier, inc=1, device_id={"seqhi": flip(hi, j)}, device_id_type=MESH)
    for j in range(1, nlo):
        pl.semaphore_signal(barrier, inc=1, device_id={"seqlo": flip(lo, j)}, device_id_type=MESH)

    inputs = (f1_in, p1_in, f2_in, p2_in)
    full = (wf1, wp1, wf2, wp2)
    local_copies = []
    for a in range(4):
        size = inputs[a].shape[0]
        here = pl.ds(pl.multiple_of(hi * size, size), size)
        local_copies.append(pltpu.make_async_copy(inputs[a], full[a].at[here], w_own.at[a]))
    mine = pl.ds(pl.multiple_of(hi * m, m), m)
    local_copies.append(pltpu.make_async_copy(x_in.at[mine], xs.at[hi], w_own.at[4]))
    local_copies.append(pltpu.make_async_copy(c_in.at[mine], cs.at[hi], w_own.at[5]))
    for copy in local_copies:
        copy.start()

    pl.semaphore_wait(barrier, nhi - 1 + nlo - 1)

    bits = []
    b = nhi // 2
    while b >= 1:
        bits.append(b)
        b //= 2
    plan = []
    held = [0]
    for b in bits:
        for h in held:
            plan.append((h, b))
        held = held + [h ^ b for h in held]

    def weight_copy(a, at):
        h, b = plan[at]
        size = inputs[a].shape[0]
        there = pl.ds(pl.multiple_of(flip(hi, h) * size, size), size)
        src = inputs[a] if h == 0 else full[a].at[there]
        return remote(src, full[a].at[there], w_send.at[a, at], w_recv.at[a, at], "seqhi", flip(hi, b))

    def sample_copy(src, dst, send, recv, j, k):
        partner = flip(hi, j)
        start = pl.multiple_of(partner * m + k * mc, mc)
        part = pl.ds(pl.multiple_of(k * mc, mc), mc)
        return remote(src.at[pl.ds(start, mc)], dst.at[hi, part], send.at[j, k], recv.at[j, k], "seqhi", partner)

    def x_copy(j, k):
        return sample_copy(x_in, xs, x_send, x_recv, j, k)

    def c_copy(j, k):
        return sample_copy(c_in, cs, c_send, c_recv, j, k)

    for a in range(4):
        for at in range(len(plan)):
            if plan[at][0] == 0:
                weight_copy(a, at).start()
    for k in range(chunks):
        for j in range(nhi - 1, 0, -1):
            x_copy(j, k).start()
        for j in range(nhi - 1, 0, -1):
            c_copy(j, k).start()

    for ref in (gf1, gp1, gf2, gp2):
        ref[...] = jnp.zeros_like(ref)
    if length > r * fcols + rp * pcols:
        g32[...] = jnp.zeros_like(g32)
        gb[...] = jnp.zeros_like(gb)

    for copy in local_copies:
        copy.wait()
    arrived = {h ^ b: at for at, (h, b) in enumerate(plan)}
    for a in range(4):
        waited = set()
        for at, (h, b) in enumerate(plan):
            if h:
                if arrived[h] not in waited:
                    weight_copy(a, arrived[h]).wait_recv()
                    waited.add(arrived[h])
                weight_copy(a, at).start()
        for at in range(len(plan)):
            if at not in waited:
                weight_copy(a, at).wait_recv()

    def gates(mixed):
        return jnp.tanh(mixed[:, :half]), sigmoid(mixed[:, half:])

    def mix(v, weight, steps):
        cut = steps * mc
        current = dot(v, weight[width:, :])
        delayed = dot(v[:-cut], weight[:width, :])
        return jnp.concatenate([current[:cut], current[cut:] + delayed], 0)

    def back(v, c, t, s, hidden, weight, projection, gf, gp, steps):
        cut = steps * mc
        dhid = dot_cols(c, projection[...])
        gp[...] += dot_rows(hidden, c)
        dmixed = jnp.concatenate(
            [dhid * s * (1.0 - t * t), dhid * t * s * (1.0 - s)], 1
        ).astype(BF16)
        gf[width:, :] += dot_rows(v, dmixed)
        gf[:width, :] += dot_rows(v[:-cut], dmixed[cut:])
        current = c.astype(F32) + dot_cols(dmixed, weight[width:, :])
        tap = dot_cols(dmixed[cut:], weight[:width, :]).astype(BF16).astype(F32)
        return jnp.concatenate([current[:-cut] + tap, current[-cut:]], 0).astype(BF16)

    rows = nhi * mc

    def y_copy(j, k):
        partner = flip(hi, j)
        start = pl.multiple_of(hi * m + k * mc, mc)
        part = pl.ds(pl.multiple_of(k * mc, mc), mc)
        return remote(
            ys.at[partner, part], y_out.at[pl.ds(start, mc)], y_send.at[j, k], y_recv.at[j, k],
            "seqhi", partner,
        )

    def y_local(k):
        start = pl.multiple_of(hi * m + k * mc, mc)
        part = pl.ds(pl.multiple_of(k * mc, mc), mc)
        return pltpu.make_async_copy(ys.at[hi, part], y_out.at[pl.ds(start, mc)], own.at[k])

    def y_start(k):
        for j in range(nhi - 1, 0, -1):
            y_copy(j, k).start()
        y_local(k).start()

    def loop(k, carry):
        part = pl.ds(pl.multiple_of(k * mc, mc), mc)
        for j in range(1, nhi):
            x_copy(j, k).wait_recv()
        x = xs[:, part, :].reshape(rows, width)
        t, s = gates(mix(x, wf1, 1))
        hidden = (t * s).astype(BF16)
        x2 = (x.astype(F32) + dot(hidden, wp1[...])).astype(BF16)
        t2, s2 = gates(mix(x2, wf2, 2))
        hidden2 = (t2 * s2).astype(BF16)
        for j in range(1, nhi):
            c_copy(j, k).wait_recv()

        c = cs[:, part, :].reshape(rows, width)
        c = back(x2, c, t2, s2, hidden2, wf2, wp2, gf2, gp2, 2)
        y = back(x, c, t, s, hidden, wf1, wp1, gf1, gp1, 1)
        ys[:, part, :] = y.reshape(nhi, mc, width)
        return carry

    lax.fori_loop(0, chunks, loop, 0)

    def pack(layer):
        gf, gp = (gf1, gp1) if layer == 0 else (gf2, gp2)
        for j in range(nhi):
            q = flip(hi, j)
            f_rows = pl.ds(pl.multiple_of(q * r, r), r)
            p_rows = pl.ds(pl.multiple_of(q * rp, rp), rp)
            for i in range(fcols + pcols):
                if i < fcols:
                    values = gf[f_rows, i * 128:(i + 1) * 128]
                    at = slice(i * r, (i + 1) * r)
                else:
                    col = i - fcols
                    values = gp[p_rows, col * 128:(col + 1) * 128]
                    at = slice(fcols * r + col * rp, fcols * r + (col + 1) * rp)
                if j & 1:
                    gb[layer, j, at, :] = values.astype(BF16)
                else:
                    g32[layer, j, at, :] = values

    def hi_copy(layer, j):
        b = j & -j
        return remote(
            gb.at[layer, j], rb.at[layer, j], h_send.at[layer, j], h_recv.at[layer, j],
            "seqhi", flip(hi, b),
        )

    def hi_slots(s):
        return [j for j in range(nhi) if j & -j == 1 << s]

    def hi_start(layer, s):
        for j in hi_slots(s):
            hi_copy(layer, j).start()

    def hi_finish(layer, s):
        for j in hi_slots(s):
            hi_copy(layer, j).wait_recv()
            target = j ^ (1 << s)
            total = g32[layer, target] + rb[layer, j].astype(F32)
            g32[layer, target] = total
            if target and target & -target == 2 << s:
                gb[layer, target] = total.astype(BF16)

    def piece_at(index):
        return pl.ds(pl.multiple_of(index * piece, piece), piece)

    def lo_copy(layer, j):
        partner = flip(lo, j)
        return remote(
            lb.at[layer, piece_at(partner)], lr.at[layer, j], l_send.at[layer, j],
            l_recv.at[layer, j], "seqlo", partner,
        )

    def lo_start(layer):
        lb[layer] = g32[layer, 0].astype(BF16)
        for j in range(nlo - 1, 0, -1):
            lo_copy(layer, j).start()

    def ag_copy(layer, j):
        return remote(
            ag.at[layer, piece_at(lo)], ag.at[layer, piece_at(lo)], a_send.at[layer, j],
            a_recv.at[layer, j], "seqlo", flip(lo, j),
        )

    def lo_finish(layer):
        total = g32[layer, 0, piece_at(lo), :]
        for j in range(1, nlo):
            lo_copy(layer, j).wait_recv()
            total = total + lr[layer, j].astype(F32)
        ag[layer, piece_at(lo), :] = (total * scale).astype(BF16)
        for j in range(nlo - 1, 0, -1):
            ag_copy(layer, j).start()

    def ag_finish(layer):
        gf, gp = (gf1_out, gp1_out) if layer == 0 else (gf2_out, gp2_out)
        for j in range(1, nlo):
            ag_copy(layer, j).wait_recv()
        for i in range(fcols):
            gf[:, i * 128:(i + 1) * 128] = ag[layer, i * r:(i + 1) * r, :].astype(F32)
        for i in range(pcols):
            at = fcols * r + i * rp
            gp[:, i * 128:(i + 1) * 128] = ag[layer, at:at + rp, :].astype(F32)

    stages = len(bits)

    def phases(layer):
        steps = []
        for s in range(stages):
            def step(s=s):
                hi_finish(layer, s)
                if s + 1 < stages:
                    hi_start(layer, s + 1)
                else:
                    lo_start(layer)
            steps.append(step)
        steps.append(lambda: lo_finish(layer))
        return steps

    for layer in (1, 0):
        pack(layer)
        hi_start(layer, 0)
    steps = [phases(1), phases(0)]
    for at in range(stages + 1):
        for side in steps:
            side[at]()
        if at == max(stages - 2, 0):
            for late in range(chunks):
                y_start(late)
    ag_finish(1)
    ag_finish(0)

    for a in range(4):
        for at in range(len(plan)):
            weight_copy(a, at).wait_send()
    for k in range(chunks):
        for j in range(1, nhi):
            x_copy(j, k).wait_send()
            c_copy(j, k).wait_send()
            y_copy(j, k).wait()
        y_local(k).wait()
    for layer in range(2):
        for j in range(1, nhi):
            hi_copy(layer, j).wait_send()
        for j in range(1, nlo):
            lo_copy(layer, j).wait_send()
            ag_copy(layer, j).wait_send()


def local(x, f1, p1, f2, p2, c):
    nhi, nlo = lax.axis_size("seqhi"), lax.axis_size("seqlo")
    samples, width = x.shape
    chunks = 4
    m = samples // nhi
    mc = m // chunks
    scale = float(samples * nhi * nlo) ** -0.5
    r, h = f1.shape
    rp = p1.shape[0]
    need = r * (h // 128) + rp * (width // 128)
    piece = -(-need // (16 * nlo)) * 16
    length = piece * nlo
    dma = pltpu.SemaphoreType.DMA
    any_spec = pl.BlockSpec(memory_space=pl.ANY)
    vmem = pl.BlockSpec(memory_space=pltpu.VMEM)
    shape = jax.ShapeDtypeStruct
    return pl.pallas_call(
        functools.partial(kernel, nhi, nlo, chunks, scale),
        out_shape=(
            shape(x.shape, BF16), shape(f1.shape, F32), shape(p1.shape, F32),
            shape(f2.shape, F32), shape(p2.shape, F32),
        ),
        in_specs=[any_spec] * 6,
        out_specs=(any_spec, vmem, vmem, vmem, vmem),
        scratch_shapes=[
            pltpu.VMEM((r * nhi, h), BF16),
            pltpu.VMEM((rp * nhi, width), BF16),
            pltpu.VMEM((r * nhi, h), BF16),
            pltpu.VMEM((rp * nhi, width), BF16),
            pltpu.VMEM((nhi, m, width), BF16),
            pltpu.VMEM((nhi, m, width), BF16),
            pltpu.VMEM((nhi, m, width), BF16),
            pltpu.VMEM((r * nhi, h), F32),
            pltpu.VMEM((rp * nhi, width), F32),
            pltpu.VMEM((r * nhi, h), F32),
            pltpu.VMEM((rp * nhi, width), F32),
            pltpu.VMEM((2, nhi, length, 128), F32),
            pltpu.VMEM((2, nhi, length, 128), BF16),
            pltpu.VMEM((2, nhi, length, 128), BF16),
            pltpu.VMEM((2, length, 128), BF16),
            pltpu.VMEM((2, nlo, piece, 128), BF16),
            pltpu.VMEM((2, length, 128), BF16),
            dma((4, nhi)), dma((4, nhi)), dma((6,)),
            dma((nhi, chunks)), dma((nhi, chunks)),
            dma((nhi, chunks)), dma((nhi, chunks)),
            dma((nhi, chunks)), dma((nhi, chunks)), dma((chunks,)),
            dma((2, nhi)), dma((2, nhi)),
            dma((2, nlo)), dma((2, nlo)),
            dma((2, nlo)), dma((2, nlo)),
        ],
        compiler_params=pltpu.CompilerParams(
            collective_id=0, has_side_effects=True, vmem_limit_bytes=62 * 1024 * 1024
        ),
        cost_estimate=pl.CostEstimate(
            flops=16 * samples * width * h * 2, bytes_accessed=8 * samples * width,
            transcendentals=4 * samples * h,
        ),
    )(x, f1, p1, f2, p2, c)


def solution(mesh):
    rows = P(("seqhi", "seqlo"), None)
    weights = P("seqhi", None)
    return jax.shard_map(
        local,
        mesh=mesh,
        in_specs=(rows, weights, weights, weights, weights, rows),
        out_specs=(rows, weights, weights, weights, weights),
        check_vma=False,
    )
```

```python
import functools

import jax
import jax.numpy as jnp
from jax import lax
from jax.experimental import pallas as pl
from jax.experimental.pallas import tpu as pltpu
from jax.sharding import PartitionSpec as P

F32, BF16 = jnp.float32, jnp.bfloat16
MESH = pl.DeviceIdType.MESH


def flip(index, bits):
    b = 1
    while b <= bits:
        if bits & b:
            index = index + b - 2 * b * lax.rem(lax.div(index, b), 2)
        b *= 2
    return index


def dot(a, b):
    return jnp.dot(a, b, preferred_element_type=F32)


def dot_rows(a, b):
    return lax.dot_general(a, b, (((0,), (0,)), ((), ())), preferred_element_type=F32)


def dot_cols(a, b):
    return lax.dot_general(a, b, (((1,), (1,)), ((), ())), preferred_element_type=F32)


def sigmoid(v):
    return 0.5 * jnp.tanh(0.5 * v) + 0.5


def kernel(
    nhi, nlo, chunks, scale,
    x_in, f1_in, p1_in, f2_in, p2_in, c_in,
    y_out, gf1_out, gp1_out, gf2_out, gp2_out,
    wf1, wp1, wf2, wp2, xs, cs, ys,
    gf1, gp1, gf2, gp2, g32, gb, rb, lb, lr, ag,
    w_send, w_recv, s_send, s_recv, w_own, x_send, x_recv, c_send, c_recv, y_send, y_recv, own,
    h_send, h_recv, l_send, l_recv, a_send, a_recv,
):
    hi, lo = lax.axis_index("seqhi"), lax.axis_index("seqlo")
    m, width = xs.shape[1], xs.shape[2]
    mc = m // chunks
    half = width
    r, rp = f1_in.shape[0], p1_in.shape[0]
    fcols, pcols = f1_in.shape[1] // 128, p1_in.shape[1] // 128
    length = g32.shape[2]
    piece = lr.shape[2]

    def remote(src, dst, send, recv, axis, partner):
        return pltpu.make_async_remote_copy(
            src_ref=src, dst_ref=dst, send_sem=send, recv_sem=recv,
            device_id={axis: partner}, device_id_type=MESH,
        )

    barrier = pltpu.get_barrier_semaphore()
    for j in range(1, nhi):
        pl.semaphore_signal(barrier, inc=1, device_id={"seqhi": flip(hi, j)}, device_id_type=MESH)
    for j in range(1, nlo):
        pl.semaphore_signal(barrier, inc=1, device_id={"seqlo": flip(lo, j)}, device_id_type=MESH)

    inputs = (f1_in, p1_in, f2_in, p2_in)
    full = (wf1, wp1, wf2, wp2)
    local_copies = []
    for a in range(4):
        size = inputs[a].shape[0]
        here = pl.ds(pl.multiple_of(hi * size, size), size)
        local_copies.append(pltpu.make_async_copy(inputs[a], full[a].at[here], w_own.at[a]))
    mine = pl.ds(pl.multiple_of(hi * m, m), m)
    local_copies.append(pltpu.make_async_copy(x_in.at[mine], xs.at[hi], w_own.at[4]))
    local_copies.append(pltpu.make_async_copy(c_in.at[mine], cs.at[hi], w_own.at[5]))
    for copy in local_copies:
        copy.start()

    pl.semaphore_wait(barrier, nhi - 1 + nlo - 1)

    bits = []
    b = nhi // 2
    while b >= 1:
        bits.append(b)
        b //= 2
    plan = []
    held = [0]
    for b in bits:
        for h in held:
            plan.append((h, b))
        held = held + [h ^ b for h in held]

    part_rows = r // nlo
    split = (0, 2) if nhi == 4 and r % (16 * nlo) == 0 else ()

    def spread_copy(a, j):
        start = pl.multiple_of(flip(hi, 2) * r + lo * part_rows, part_rows)
        there = full[a].at[pl.ds(start, part_rows)]
        return remote(there, there, s_send.at[a, j], s_recv.at[a, j], "seqlo", flip(lo, j))

    def weight_copy(a, at):
        h, b = plan[at]
        size = inputs[a].shape[0]
        there = pl.ds(pl.multiple_of(flip(hi, h) * size, size), size)
        src = inputs[a] if h == 0 else full[a].at[there]
        if a in split and at == 0:
            src = inputs[a].at[pl.ds(pl.multiple_of(lo * part_rows, part_rows), part_rows)]
            start = pl.multiple_of(hi * size + lo * part_rows, part_rows)
            there = pl.ds(start, part_rows)
        return remote(src, full[a].at[there], w_send.at[a, at], w_recv.at[a, at], "seqhi", flip(hi, b))

    def sample_copy(src, dst, send, recv, j, k):
        partner = flip(hi, j)
        start = pl.multiple_of(partner * m + k * mc, mc)
        part = pl.ds(pl.multiple_of(k * mc, mc), mc)
        return remote(src.at[pl.ds(start, mc)], dst.at[hi, part], send.at[j, k], recv.at[j, k], "seqhi", partner)

    def x_copy(j, k):
        return sample_copy(x_in, xs, x_send, x_recv, j, k)

    def c_copy(j, k):
        return sample_copy(c_in, cs, c_send, c_recv, j, k)

    for a in (0, 2, 1, 3):
        for at in range(len(plan)):
            if plan[at][0] == 0:
                weight_copy(a, at).start()
    for k in range(chunks):
        for j in (*range(2, nhi), 1):
            x_copy(j, k).start()
        for j in (*range(2, nhi), 1):
            c_copy(j, k).start()

    for a in split:
        weight_copy(a, 0).wait_recv()
        for j in range(nlo - 1, 0, -1):
            spread_copy(a, j).start()

    for ref in (gf1, gp1, gf2, gp2):
        ref[...] = jnp.zeros_like(ref)
    if length > r * fcols + rp * pcols:
        g32[...] = jnp.zeros_like(g32)
        gb[...] = jnp.zeros_like(gb)

    for copy in local_copies:
        copy.wait()
    unread = []
    arrived = {h ^ b: at for at, (h, b) in enumerate(plan)}
    for a in range(4):
        waited = set()
        if a in split:
            waited.add(0)
            for j in range(1, nlo):
                spread_copy(a, j).wait_recv()
        for at, (h, b) in enumerate(plan):
            if h:
                if arrived[h] not in waited:
                    weight_copy(a, arrived[h]).wait_recv()
                    waited.add(arrived[h])
                weight_copy(a, at).start()
        for at in range(len(plan)):
            if at not in waited:
                unread.append((a, at))
    for a, at in unread:
        weight_copy(a, at).wait_recv()

    def gates(mixed):
        return jnp.tanh(mixed[:, :half]), sigmoid(mixed[:, half:])

    def mix(v, weight, steps):
        cut = steps * mc
        current = dot(v, weight[width:, :])
        delayed = dot(v[:-cut], weight[:width, :])
        return jnp.concatenate([current[:cut], current[cut:] + delayed], 0)

    def back(v, c, t, s, hidden, weight, projection, gf, gp, steps):
        cut = steps * mc
        dhid = dot_cols(c, projection[...])
        gp[...] += dot_rows(hidden, c)
        dmixed = jnp.concatenate(
            [dhid * s * (1.0 - t * t), dhid * t * s * (1.0 - s)], 1
        ).astype(BF16)
        gf[width:, :] += dot_rows(v, dmixed)
        gf[:width, :] += dot_rows(v[:-cut], dmixed[cut:])
        current = c.astype(F32) + dot_cols(dmixed, weight[width:, :])
        tap = dot_cols(dmixed[cut:], weight[:width, :]).astype(BF16).astype(F32)
        return jnp.concatenate([current[:-cut] + tap, current[-cut:]], 0).astype(BF16)

    rows = nhi * mc

    def y_copy(j, k):
        partner = flip(hi, j)
        start = pl.multiple_of(hi * m + k * mc, mc)
        part = pl.ds(pl.multiple_of(k * mc, mc), mc)
        return remote(
            ys.at[partner, part], y_out.at[pl.ds(start, mc)], y_send.at[j, k], y_recv.at[j, k],
            "seqhi", partner,
        )

    def y_local(k):
        start = pl.multiple_of(hi * m + k * mc, mc)
        part = pl.ds(pl.multiple_of(k * mc, mc), mc)
        return pltpu.make_async_copy(ys.at[hi, part], y_out.at[pl.ds(start, mc)], own.at[k])

    def y_start(k):
        for j in range(nhi - 1, 0, -1):
            y_copy(j, k).start()
        y_local(k).start()

    def loop(k, carry):
        part = pl.ds(pl.multiple_of(k * mc, mc), mc)
        for j in range(1, nhi):
            x_copy(j, k).wait_recv()
        x = xs[:, part, :].reshape(rows, width)
        t, s = gates(mix(x, wf1, 1))
        hidden = (t * s).astype(BF16)
        x2 = (x.astype(F32) + dot(hidden, wp1[...])).astype(BF16)
        t2, s2 = gates(mix(x2, wf2, 2))
        hidden2 = (t2 * s2).astype(BF16)
        for j in range(1, nhi):
            c_copy(j, k).wait_recv()

        c = cs[:, part, :].reshape(rows, width)
        c = back(x2, c, t2, s2, hidden2, wf2, wp2, gf2, gp2, 2)
        y = back(x, c, t, s, hidden, wf1, wp1, gf1, gp1, 1)
        ys[:, part, :] = y.reshape(nhi, mc, width)
        return carry

    lax.fori_loop(0, chunks, loop, 0)

    def pack(layer):
        gf, gp = (gf1, gp1) if layer == 0 else (gf2, gp2)
        for j in range(nhi):
            q = flip(hi, j)
            f_rows = pl.ds(pl.multiple_of(q * r, r), r)
            p_rows = pl.ds(pl.multiple_of(q * rp, rp), rp)
            for i in range(fcols + pcols):
                if i < fcols:
                    values = gf[f_rows, i * 128:(i + 1) * 128]
                    at = slice(i * r, (i + 1) * r)
                else:
                    col = i - fcols
                    values = gp[p_rows, col * 128:(col + 1) * 128]
                    at = slice(fcols * r + col * rp, fcols * r + (col + 1) * rp)
                if j & 1:
                    gb[layer, j, at, :] = values.astype(BF16)
                else:
                    g32[layer, j, at, :] = values

    def hi_copy(layer, j):
        b = j & -j
        return remote(
            gb.at[layer, j], rb.at[layer, j], h_send.at[layer, j], h_recv.at[layer, j],
            "seqhi", flip(hi, b),
        )

    def hi_slots(s):
        return [j for j in range(nhi) if j & -j == 1 << s]

    def hi_start(layer, s):
        for j in hi_slots(s):
            hi_copy(layer, j).start()

    def hi_finish(layer, s):
        for j in hi_slots(s):
            hi_copy(layer, j).wait_recv()
            target = j ^ (1 << s)
            total = g32[layer, target] + rb[layer, j].astype(F32)
            g32[layer, target] = total
            if target and target & -target == 2 << s:
                gb[layer, target] = total.astype(BF16)

    def piece_at(index):
        return pl.ds(pl.multiple_of(index * piece, piece), piece)

    def lo_copy(layer, j):
        partner = flip(lo, j)
        return remote(
            lb.at[layer, piece_at(partner)], lr.at[layer, j], l_send.at[layer, j],
            l_recv.at[layer, j], "seqlo", partner,
        )

    def lo_start(layer):
        lb[layer] = g32[layer, 0].astype(BF16)
        for j in range(nlo - 1, 0, -1):
            lo_copy(layer, j).start()

    def ag_copy(layer, j):
        return remote(
            ag.at[layer, piece_at(lo)], ag.at[layer, piece_at(lo)], a_send.at[layer, j],
            a_recv.at[layer, j], "seqlo", flip(lo, j),
        )

    def lo_finish(layer):
        total = g32[layer, 0, piece_at(lo), :]
        for j in range(1, nlo):
            lo_copy(layer, j).wait_recv()
            total = total + lr[layer, j].astype(F32)
        ag[layer, piece_at(lo), :] = (total * scale).astype(BF16)
        for j in range(nlo - 1, 0, -1):
            ag_copy(layer, j).start()

    def ag_finish(layer):
        gf, gp = (gf1_out, gp1_out) if layer == 0 else (gf2_out, gp2_out)
        for j in range(1, nlo):
            ag_copy(layer, j).wait_recv()
        for i in range(fcols):
            gf[:, i * 128:(i + 1) * 128] = ag[layer, i * r:(i + 1) * r, :].astype(F32)
        for i in range(pcols):
            at = fcols * r + i * rp
            gp[:, i * 128:(i + 1) * 128] = ag[layer, at:at + rp, :].astype(F32)

    stages = len(bits)

    def phases(layer):
        steps = []
        for s in range(stages):
            def step(s=s):
                hi_finish(layer, s)
                if s + 1 < stages:
                    hi_start(layer, s + 1)
                else:
                    lo_start(layer)
            steps.append(step)
        steps.append(lambda: lo_finish(layer))
        return steps

    for layer in (1, 0):
        pack(layer)
        hi_start(layer, 0)
    steps = [phases(1), phases(0)]
    for at in range(stages + 1):
        for side in steps:
            side[at]()
        if at == max(stages - 2, 0):
            for late in range(chunks):
                y_start(late)
    ag_finish(1)
    ag_finish(0)

    for a in range(4):
        for at in range(len(plan)):
            weight_copy(a, at).wait_send()
    for a in split:
        for j in range(1, nlo):
            spread_copy(a, j).wait_send()
    for k in range(chunks):
        for j in range(1, nhi):
            x_copy(j, k).wait_send()
            c_copy(j, k).wait_send()
            y_copy(j, k).wait()
        y_local(k).wait()
    for layer in range(2):
        for j in range(1, nhi):
            hi_copy(layer, j).wait_send()
        for j in range(1, nlo):
            lo_copy(layer, j).wait_send()
            ag_copy(layer, j).wait_send()


def local(x, f1, p1, f2, p2, c):
    nhi, nlo = lax.axis_size("seqhi"), lax.axis_size("seqlo")
    samples, width = x.shape
    chunks = 4
    m = samples // nhi
    mc = m // chunks
    scale = float(samples * nhi * nlo) ** -0.5
    r, h = f1.shape
    rp = p1.shape[0]
    need = r * (h // 128) + rp * (width // 128)
    piece = -(-need // (16 * nlo)) * 16
    length = piece * nlo
    dma = pltpu.SemaphoreType.DMA
    any_spec = pl.BlockSpec(memory_space=pl.ANY)
    vmem = pl.BlockSpec(memory_space=pltpu.VMEM)
    shape = jax.ShapeDtypeStruct
    return pl.pallas_call(
        functools.partial(kernel, nhi, nlo, chunks, scale),
        out_shape=(
            shape(x.shape, BF16), shape(f1.shape, F32), shape(p1.shape, F32),
            shape(f2.shape, F32), shape(p2.shape, F32),
        ),
        in_specs=[any_spec] * 6,
        out_specs=(any_spec, vmem, vmem, vmem, vmem),
        scratch_shapes=[
            pltpu.VMEM((r * nhi, h), BF16),
            pltpu.VMEM((rp * nhi, width), BF16),
            pltpu.VMEM((r * nhi, h), BF16),
            pltpu.VMEM((rp * nhi, width), BF16),
            pltpu.VMEM((nhi, m, width), BF16),
            pltpu.VMEM((nhi, m, width), BF16),
            pltpu.VMEM((nhi, m, width), BF16),
            pltpu.VMEM((r * nhi, h), F32),
            pltpu.VMEM((rp * nhi, width), F32),
            pltpu.VMEM((r * nhi, h), F32),
            pltpu.VMEM((rp * nhi, width), F32),
            pltpu.VMEM((2, nhi, length, 128), F32),
            pltpu.VMEM((2, nhi, length, 128), BF16),
            pltpu.VMEM((2, nhi, length, 128), BF16),
            pltpu.VMEM((2, length, 128), BF16),
            pltpu.VMEM((2, nlo, piece, 128), BF16),
            pltpu.VMEM((2, length, 128), BF16),
            dma((4, nhi)), dma((4, nhi)), dma((4, nlo)), dma((4, nlo)), dma((6,)),
            dma((nhi, chunks)), dma((nhi, chunks)),
            dma((nhi, chunks)), dma((nhi, chunks)),
            dma((nhi, chunks)), dma((nhi, chunks)), dma((chunks,)),
            dma((2, nhi)), dma((2, nhi)),
            dma((2, nlo)), dma((2, nlo)),
            dma((2, nlo)), dma((2, nlo)),
        ],
        compiler_params=pltpu.CompilerParams(
            collective_id=0, has_side_effects=True, vmem_limit_bytes=62 * 1024 * 1024
        ),
        cost_estimate=pl.CostEstimate(
            flops=16 * samples * width * h * 2, bytes_accessed=8 * samples * width,
            transcendentals=4 * samples * h,
        ),
    )(x, f1, p1, f2, p2, c)


def solution(mesh):
    rows = P(("seqhi", "seqlo"), None)
    weights = P("seqhi", None)
    return jax.shard_map(
        local,
        mesh=mesh,
        in_specs=(rows, weights, weights, weights, weights, rows),
        out_specs=(rows, weights, weights, weights, weights),
        check_vma=False,
    )
```
